32 devices in a mesh: tm: 4 (over y, core), chan: 4 (over z), stn: 2 (over x).
Axes of the slice: x: 2, y: 2, z: 4, core: 2. Of those that a mesh axis runs over, the one named last changes fastest.
Arguments:
- voltages: bfloat16 [2, 64, 768, 4096], P(None, 'tm', ('chan', 'stn')), may hold values from -6 to 6
- coefficients: float32 [16, 4096], replicated, may hold values from -2.5 to 2.5
- kept_channels: int32 [384], replicated, may hold values from 0 to 4095, as said below
- station_flags: int32 [768], P(('chan', 'stn')), may hold values 0 or 1
Outputs:
- visibilities: float32 [2, 384, 768, 768], P(None, 'chan', ('tm', 'stn'))
The draws below stay inside these ranges and needn't reach their ends.
Inputs may be any that keep to these rules, and one draw needn't show every extreme that they name: `kept_channels`: 384 distinct channel numbers, in no particular order.
All inputs are finite; a program needn't handle non-finite values. No bound on the sum of `station_flags` on one device may be relied on, other than what follows from the above.
Results may differ from the reference program's by a relative error of at most 0.0039.
Values may be sent and summed in bfloat16 or wider, within the bound.
A program may use at most 256 MiB of HBM per device.

```python
import math
import jax
import jax.numpy as jnp
from jax import lax

NFFT = 4096
TAPS = 16
KEPT = 384
INPUTS = 768
FRAMES = 64


def draw_kept_channels(key, part):
    key = jax.random.fold_in(key, 5)
    first_key, second_key = jax.random.split(key)
    inner = jax.random.permutation(first_key, NFFT - 2)[:KEPT - 2] + 1
    ends = jnp.array([0, NFFT - 1], dtype=jnp.int32)
    chosen = jnp.concatenate([ends, inner.astype(jnp.int32)])
    return jax.random.permutation(second_key, chosen).astype(jnp.int32)


def plant(values, key, low, largest):
    dims = values.shape
    index_at = [jax.random.randint(jax.random.fold_in(key, axis), (), 0, dims[axis]) for axis in range(len(dims))]
    values = values.at[tuple(index_at)].set(low)
    longest = dims.index(max(dims))
    index_at[longest] = (index_at[longest] + 1) % dims[longest]
    return values.at[tuple(index_at)].set(largest)


def levels(key, dims, cuts, low, top_value):
    level = 1.0
    for position, shards_of in cuts:
        steps = jax.random.uniform(jax.random.fold_in(jax.random.fold_in(key, 6), position), (shards_of,), jnp.float32, low / len(cuts), top_value / len(cuts))
        level = level * jnp.repeat(jnp.exp(steps), dims[position] // shards_of).reshape((-1,) + (1,) * (len(dims) - 1 - position))
    return level


def scatter_about(stream_key, extent, width, bound, shards=(), held_as=jnp.bfloat16):
    drawn = width * jax.random.normal(stream_key, extent, jnp.float32)
    if shards:
        drawn = drawn * levels(stream_key, extent, shards, -0.22, 0.18)
    return jnp.clip(drawn, -bound, bound).astype(held_as)


def setup_inputs(seed: int = 0) -> dict:
    seeds = jax.random.split(jax.random.key(seed), 5)
    return {
        "voltages": scatter_about(seeds[0], (2, FRAMES, INPUTS, NFFT), 1.0, 6.0, ((1, 4), (2, 8))),
        "coefficients": scatter_about(seeds[1], (TAPS, NFFT), 0.25, 2.5, (), jnp.float32),
        "kept_channels": draw_kept_channels(jax.random.fold_in(seeds[4], 71), 0),
        "station_flags": plant((jax.random.randint(seeds[3], (INPUTS,), 0, 8) < 7).astype(jnp.int32), jax.random.fold_in(seeds[3], 1), 0, 1),
    }


def build_tables(kept_channels, nfft_length):
    positions = jnp.arange(nfft_length, dtype=jnp.int32)
    phases = positions[:, None] * kept_channels[None, :].astype(jnp.int32) % nfft_length
    angles = phases.astype(jnp.float32) * (2.0 * math.pi / nfft_length)
    normalizer = 1.0 / math.sqrt(nfft_length)
    return (jnp.cos(angles) * normalizer, jnp.sin(angles) * normalizer)

def tap_sum(extended, coefficients, frame_count):
    tap_count = coefficients.shape[0]
    total = coefficients[0][None, None, None, :] * extended[:, tap_count - 1:tap_count - 1 + frame_count]
    for tap_index in range(1, tap_count):
        first = tap_count - 1 - tap_index
        total = total + coefficients[tap_index][None, None, None, :] * extended[:, first:first + frame_count]
    return total

def transform(filtered, cosine_table, sine_table):
    highest = lax.Precision.HIGHEST
    real_part = jnp.einsum('fin,nk->kif', filtered[0], cosine_table, precision=highest, preferred_element_type=jnp.float32) + jnp.einsum('fin,nk->kif', filtered[1], sine_table, precision=highest, preferred_element_type=jnp.float32)
    imag_part = jnp.einsum('fin,nk->kif', filtered[1], cosine_table, precision=highest, preferred_element_type=jnp.float32) - jnp.einsum('fin,nk->kif', filtered[0], sine_table, precision=highest, preferred_element_type=jnp.float32)
    return (real_part, imag_part)

def reference(voltages, coefficients, kept_channels, station_flags):
    cosine_table, sine_table = build_tables(kept_channels, NFFT)
    group_size = math.gcd(INPUTS, 64)

    def channelize(offset):
        samples = lax.dynamic_slice_in_dim(voltages, offset, group_size, 2).astype(jnp.float32)
        leading = jnp.zeros((2, TAPS - 1, group_size, NFFT), jnp.float32)
        filtered = tap_sum(jnp.concatenate([leading, samples], axis=1), coefficients, FRAMES)
        real_part, imag_part = transform(filtered, cosine_table, sine_table)
        weights = lax.dynamic_slice_in_dim(station_flags, offset, group_size, 0).astype(jnp.float32)
        return (jnp.stack([real_part, imag_part]) * weights[None, None, :, None]).astype(jnp.bfloat16)
    offsets = jnp.arange(0, INPUTS, group_size, dtype=jnp.int32)
    grouped = lax.map(channelize, offsets)
    spectra = jnp.transpose(grouped, (1, 2, 0, 3, 4)).reshape(2, KEPT, INPUTS, FRAMES)
    by_channel = jnp.transpose(spectra, (1, 0, 2, 3))

    def correlate_one(channel):
        real_rows = channel[0]
        imag_rows = channel[1]
        real_vis = jnp.dot(real_rows, real_rows.T, preferred_element_type=jnp.float32) + jnp.dot(imag_rows, imag_rows.T, preferred_element_type=jnp.float32)
        imag_vis = jnp.dot(imag_rows, real_rows.T, preferred_element_type=jnp.float32) - jnp.dot(real_rows, imag_rows.T, preferred_element_type=jnp.float32)
        return jnp.stack([real_vis, imag_vis]) * (1.0 / FRAMES)
    result = lax.map(correlate_one, by_channel)
    return jnp.transpose(result, (1, 0, 2, 3))
```

```python
import math

import jax
import jax.numpy as jnp
from jax import lax
from jax.experimental import pallas as pl
from jax.experimental.pallas import tpu as pltpu
from jax.sharding import PartitionSpec as P

GROUP = 16
LANES = 128
CHUNK = 512


def passed_along(block, axis, distance):
    devices = range(lax.axis_size(axis))
    route = [(i - distance, i) for i in devices if i - distance in devices]
    return lax.ppermute(block, axis, route)


def build_table(kept_channels, nfft_length):
    positions = jnp.arange(nfft_length, dtype=jnp.int32)
    phases = positions[:, None] * kept_channels[None, :] % nfft_length
    angles = phases.astype(jnp.float32) * (2.0 * math.pi / nfft_length)
    normalizer = 1.0 / math.sqrt(nfft_length)
    return jnp.concatenate([jnp.cos(angles) * normalizer, jnp.sin(angles) * normalizer], axis=1)


def tap_sum(extended, coefficients, frame_count):
    tap_count = coefficients.shape[0]
    start = tap_count - 1
    total = coefficients[0][None, None, None, :] * extended[:, start : start + frame_count].astype(
        jnp.float32
    )
    for tap_index in range(1, tap_count):
        first = tap_count - 1 - tap_index
        total = total + coefficients[tap_index][None, None, None, :] * extended[
            :, first : first + frame_count
        ].astype(jnp.float32)
    return total


def transform(filtered, joint_table, channel_count):
    product = jnp.einsum(
        "pfin,nk->pkif",
        filtered,
        joint_table,
        precision=lax.Precision.HIGHEST,
        preferred_element_type=jnp.float32,
    )
    real_part = product[0, :channel_count] + product[1, channel_count:]
    imag_part = product[1, :channel_count] - product[0, channel_count:]
    return (real_part, imag_part)


def correlate(spectra_all, row_start, row_count):
    mine = lax.dynamic_slice_in_dim(spectra_all, row_start, row_count, 2)
    left_side = jnp.stack(
        [
            jnp.concatenate([mine[0], mine[1]], axis=-1),
            jnp.concatenate([mine[1], -mine[0]], axis=-1),
        ]
    )
    right_side = jnp.concatenate([spectra_all[0], spectra_all[1]], axis=-1)
    return jnp.einsum("pcif,cjf->pcij", left_side, right_side, preferred_element_type=jnp.float32)


def plain_shards(voltages, coefficients, kept_channels, station_flags):
    frames_dev = voltages.shape[1]
    inputs_dev = voltages.shape[2]
    nfft_length = voltages.shape[3]
    tap_count = coefficients.shape[0]
    channel_count = kept_channels.shape[0]
    history = tap_count - 1
    joint_table = build_table(kept_channels, nfft_length)
    trailing = voltages[:, frames_dev - history :]
    earlier = passed_along(trailing, "tm", 1)
    extended = jnp.concatenate([earlier, voltages], axis=1)
    filtered = tap_sum(extended, coefficients, frames_dev)
    real_part, imag_part = transform(filtered, joint_table, channel_count)
    weights = station_flags.astype(jnp.float32)
    spectra = (jnp.stack([real_part, imag_part]) * weights[None, None, :, None]).astype(
        jnp.bfloat16
    )
    local_spectra = spectra.reshape(2, channel_count, 1, 1, inputs_dev, frames_dev)
    turned = lax.all_to_all(local_spectra, "chan", split_axis=1, concat_axis=2, tiled=True)
    n_time = lax.axis_size("tm")
    n_station = lax.axis_size("stn")
    owned = turned.shape[1]
    groups = turned.shape[2]
    inputs_total = groups * n_station * inputs_dev
    row_count = inputs_total // (n_time * n_station)
    row_start = (lax.axis_index("tm") * n_station + lax.axis_index("stn")) * row_count
    frames_total = frames_dev * n_time
    everything = lax.all_gather(turned[None], ("tm", "stn"), axis=0, tiled=True)
    everything = everything.reshape(n_time, n_station, 2, owned, groups, inputs_dev, frames_dev)
    spectra_all = jnp.transpose(everything, (2, 3, 4, 1, 5, 0, 6)).reshape(
        2, owned, inputs_total, frames_total
    )
    summed = correlate(spectra_all, row_start, row_count)
    return summed * (1.0 / frames_total)


def build_blocks(kept_channels, nfft_length):
    low_count = 64
    high = jnp.arange(nfft_length // low_count, dtype=jnp.int32) * low_count
    low = jnp.arange(low_count, dtype=jnp.int32)
    step = 2.0 * math.pi / nfft_length

    def waves(positions):
        phases = kept_channels[:, None] * positions[None, :] % nfft_length
        angles = phases.astype(jnp.float32) * step
        return jnp.cos(angles), jnp.sin(angles)

    high_cos, high_sin = waves(high)
    low_cos, low_sin = waves(low)
    expand = lambda x: jnp.repeat(x, low_count, axis=1)
    spread = lambda x: jnp.tile(x, (1, nfft_length // low_count))
    hc, hs, lc, ls = expand(high_cos), expand(high_sin), spread(low_cos), spread(low_sin)
    normalizer = 1.0 / math.sqrt(nfft_length)
    cosine = ((hc * lc - hs * ls) * normalizer).astype(jnp.bfloat16)
    sine = ((hs * lc + hc * ls) * normalizer).astype(jnp.bfloat16)
    return jnp.stack([jnp.stack([cosine, sine]), jnp.stack([-sine, cosine])])


def channelize_body(later, v_ref, c_ref, t_ref, out_ref, even, odd):
    step = pl.program_id(0)
    frames, inputs = v_ref.shape[1], v_ref.shape[2]
    taps = c_ref.shape[0]
    channels = t_ref.shape[2]
    width = v_ref.shape[3]
    pieces = inputs // GROUP
    piece = frames * GROUP

    def phase(filling, reading):
        def part(s, carry):
            row = pl.multiple_of(s * GROUP, GROUP)
            for p in range(2):
                for lane in range(0, width, LANES):
                    at = slice(lane, lane + LANES)
                    v = [
                        v_ref[p, f, pl.ds(row, GROUP), at].astype(jnp.float32)
                        for f in range(frames)
                    ]
                    c = [c_ref[t : t + 1, at] for t in range(taps)]
                    for f in range(frames):
                        total = None
                        for t in range(taps):
                            source = f - t + (frames if later else 0)
                            if 0 <= source < frames:
                                term = c[t] * v[source]
                                total = term if total is None else total + term
                        if total is None:
                            total = jnp.zeros((GROUP, LANES), jnp.float32)
                        upper = total.astype(jnp.bfloat16)
                        lower = (total - upper.astype(jnp.float32)).astype(jnp.bfloat16)
                        place = pl.ds(pl.multiple_of(f * inputs + row, GROUP), GROUP)
                        filling[2 * p, place, at] = upper
                        filling[2 * p + 1, place, at] = lower
            rows = pl.ds(pl.multiple_of(s * piece, LANES), piece)
            for h in range(2):
                total = None
                for p in range(2):
                    for q in range(2):
                        term = lax.dot_general(
                            t_ref[h, p],
                            reading[2 * p + q, rows, :],
                            (((1,), (1,)), ((), ())),
                            preferred_element_type=jnp.float32,
                        )
                        total = term if total is None else total + term
                before = out_ref[h, :, rows]
                out_ref[h, :, rows] = jnp.where(step <= 1, 0.0, before) + total
            return carry

        lax.fori_loop(0, pieces, part, 0)

    @pl.when(step % 2 == 0)
    def _():
        phase(even, odd)

    @pl.when(step % 2 == 1)
    def _():
        phase(odd, even)


def channelize(voltages, coefficients, blocks, later):
    _, frames, inputs, nfft_length = voltages.shape
    taps = coefficients.shape[0]
    channels = blocks.shape[2]
    rows = frames * inputs
    chunks = nfft_length // CHUNK
    last = chunks - 1
    return pl.pallas_call(
        lambda *refs: channelize_body(later, *refs),
        grid=(chunks + 1,),
        in_specs=[
            pl.BlockSpec((2, frames, inputs, CHUNK), lambda j: (0, 0, 0, jnp.minimum(j, last))),
            pl.BlockSpec((taps, CHUNK), lambda j: (0, jnp.minimum(j, last))),
            pl.BlockSpec((2, 2, channels, CHUNK), lambda j: (0, 0, 0, jnp.maximum(j - 1, 0))),
        ],
        out_specs=pl.BlockSpec((2, channels, rows), lambda j: (0, 0, 0)),
        out_shape=jax.ShapeDtypeStruct((2, channels, rows), jnp.float32),
        scratch_shapes=[pltpu.VMEM((4, rows, CHUNK), jnp.bfloat16)] * 2,
        compiler_params=pltpu.CompilerParams(vmem_limit_bytes=56 * 1024 * 1024),
        cost_estimate=pl.CostEstimate(
            flops=16 * rows * channels * nfft_length, bytes_accessed=60_000_000, transcendentals=0
        ),
    )(voltages, coefficients, blocks)


def correlate_body(scale, which_ref, s_ref, out_ref):
    n_time, n_station, _, count, frames, width = s_ref.shape
    inputs = out_ref.shape[2]
    groups = width // inputs
    which = which_ref[0]
    for k in range(count):
        parts = []
        for station in range(n_station):
            parts.append(
                jnp.concatenate(
                    [s_ref[t, station, p, k] for p in range(2) for t in range(n_time)], axis=0
                )
            )
        cuts = [
            parts[station][:, g * inputs : (g + 1) * inputs]
            for g in range(groups)
            for station in range(n_station)
        ]
        right = jnp.concatenate(cuts, axis=1)
        mine = cuts[0]
        for index in range(1, len(cuts)):
            mine = jnp.where(which == index, cuts[index], mine)
        half = mine.shape[0] // 2
        turned = jnp.concatenate([mine[half:], -mine[:half]], axis=0)
        for h, left in enumerate((mine, turned)):
            product = lax.dot_general(
                left, right, (((0,), (0,)), ((), ())), preferred_element_type=jnp.float32
            )
            out_ref[h, k] = product * scale


def correlate_all(everything, which, inputs, scale):
    n_time, n_station, _, owned, frames, width = everything.shape
    count = 4
    total = n_station * width
    return pl.pallas_call(
        lambda *refs: correlate_body(scale, *refs),
        grid=(owned // count,),
        in_specs=[
            pl.BlockSpec(memory_space=pltpu.SMEM),
            pl.BlockSpec(
                (n_time, n_station, 2, count, frames, width), lambda j: (0, 0, 0, j, 0, 0)
            ),
        ],
        out_specs=pl.BlockSpec((2, count, inputs, total), lambda j: (0, j, 0, 0)),
        out_shape=jax.ShapeDtypeStruct((2, owned, inputs, total), jnp.float32),
        compiler_params=pltpu.CompilerParams(vmem_limit_bytes=48 * 1024 * 1024),
    )(which, everything)


def shards(voltages, coefficients, kept_channels, station_flags):
    _, frames, inputs, nfft_length = voltages.shape
    channels = kept_channels.shape[0]
    n_time, n_station, n_chan = (lax.axis_size(a) for a in ("tm", "stn", "chan"))
    fits = (
        inputs % GROUP == 0
        and frames % 16 == 0
        and coefficients.shape[0] <= frames + 1
        and nfft_length % CHUNK == 0
        and frames * GROUP % LANES == 0
        and n_chan * n_station == n_time * n_station
        and n_chan * inputs % LANES == 0
        and channels // n_chan % 4 == 0
    )
    if not fits:
        return plain_shards(voltages, coefficients, kept_channels, station_flags)
    blocks = build_blocks(kept_channels, nfft_length)
    after = channelize(voltages, coefficients, blocks, True)
    earlier = passed_along(after, "tm", 1)
    own = channelize(voltages, coefficients, blocks, False)
    weights = jnp.tile(station_flags.astype(jnp.float32), frames)
    spectra = ((own + earlier) * weights).astype(jnp.bfloat16)
    owned = channels // n_chan
    spectra = spectra.reshape(2, n_chan, owned, frames, inputs)
    turned = lax.all_to_all(spectra, "chan", split_axis=1, concat_axis=1, tiled=True)
    merged = jnp.transpose(turned, (0, 2, 3, 1, 4)).reshape(2, owned, frames, n_chan * inputs)
    everything = lax.all_gather(merged[None], ("tm", "stn"), axis=0, tiled=True)
    everything = everything.reshape(n_time, n_station, *merged.shape)
    which = lax.axis_index("tm") * n_station + lax.axis_index("stn")
    scale = 1.0 / (frames * n_time)
    return correlate_all(everything, which.astype(jnp.int32)[None], inputs, scale)


def solution(mesh):
    placed = (P(None, "tm", ("chan", "stn"), None), P(), P(), P(("chan", "stn")))
    return jax.shard_map(
        shards,
        mesh=mesh,
        in_specs=placed,
        out_specs=P(None, "chan", ("tm", "stn"), None),
        check_vma=False,
    )
```

```python
import math

import jax
import jax.numpy as jnp
from jax import lax
from jax.experimental import pallas as pl
from jax.experimental.pallas import tpu as pltpu
from jax.sharding import PartitionSpec as P

GROUP = 16
LANES = 128
CHUNK = 512


def passed_along(block, axis, distance):
    devices = range(lax.axis_size(axis))
    route = [(i - distance, i) for i in devices if i - distance in devices]
    return lax.ppermute(block, axis, route)


def build_table(kept_channels, nfft_length):
    positions = jnp.arange(nfft_length, dtype=jnp.int32)
    phases = positions[:, None] * kept_channels[None, :] % nfft_length
    angles = phases.astype(jnp.float32) * (2.0 * math.pi / nfft_length)
    normalizer = 1.0 / math.sqrt(nfft_length)
    return jnp.concatenate([jnp.cos(angles) * normalizer, jnp.sin(angles) * normalizer], axis=1)


def tap_sum(extended, coefficients, frame_count):
    tap_count = coefficients.shape[0]
    start = tap_count - 1
    total = coefficients[0][None, None, None, :] * extended[:, start : start + frame_count].astype(
        jnp.float32
    )
    for tap_index in range(1, tap_count):
        first = tap_count - 1 - tap_index
        total = total + coefficients[tap_index][None, None, None, :] * extended[
            :, first : first + frame_count
        ].astype(jnp.float32)
    return total


def transform(filtered, joint_table, channel_count):
    product = jnp.einsum(
        "pfin,nk->pkif",
        filtered,
        joint_table,
        precision=lax.Precision.HIGHEST,
        preferred_element_type=jnp.float32,
    )
    real_part = product[0, :channel_count] + product[1, channel_count:]
    imag_part = product[1, :channel_count] - product[0, channel_count:]
    return (real_part, imag_part)


def correlate(spectra_all, row_start, row_count):
    mine = lax.dynamic_slice_in_dim(spectra_all, row_start, row_count, 2)
    left_side = jnp.stack(
        [
            jnp.concatenate([mine[0], mine[1]], axis=-1),
            jnp.concatenate([mine[1], -mine[0]], axis=-1),
        ]
    )
    right_side = jnp.concatenate([spectra_all[0], spectra_all[1]], axis=-1)
    return jnp.einsum("pcif,cjf->pcij", left_side, right_side, preferred_element_type=jnp.float32)


def plain_shards(voltages, coefficients, kept_channels, station_flags):
    frames_dev = voltages.shape[1]
    inputs_dev = voltages.shape[2]
    nfft_length = voltages.shape[3]
    tap_count = coefficients.shape[0]
    channel_count = kept_channels.shape[0]
    history = tap_count - 1
    joint_table = build_table(kept_channels, nfft_length)
    trailing = voltages[:, frames_dev - history :]
    earlier = passed_along(trailing, "tm", 1)
    extended = jnp.concatenate([earlier, voltages], axis=1)
    filtered = tap_sum(extended, coefficients, frames_dev)
    real_part, imag_part = transform(filtered, joint_table, channel_count)
    weights = station_flags.astype(jnp.float32)
    spectra = (jnp.stack([real_part, imag_part]) * weights[None, None, :, None]).astype(
        jnp.bfloat16
    )
    local_spectra = spectra.reshape(2, channel_count, 1, 1, inputs_dev, frames_dev)
    turned = lax.all_to_all(local_spectra, "chan", split_axis=1, concat_axis=2, tiled=True)
    n_time = lax.axis_size("tm")
    n_station = lax.axis_size("stn")
    owned = turned.shape[1]
    groups = turned.shape[2]
    inputs_total = groups * n_station * inputs_dev
    row_count = inputs_total // (n_time * n_station)
    row_start = (lax.axis_index("tm") * n_station + lax.axis_index("stn")) * row_count
    frames_total = frames_dev * n_time
    everything = lax.all_gather(turned[None], ("tm", "stn"), axis=0, tiled=True)
    everything = everything.reshape(n_time, n_station, 2, owned, groups, inputs_dev, frames_dev)
    spectra_all = jnp.transpose(everything, (2, 3, 4, 1, 5, 0, 6)).reshape(
        2, owned, inputs_total, frames_total
    )
    summed = correlate(spectra_all, row_start, row_count)
    return summed * (1.0 / frames_total)


def build_blocks(kept_channels, nfft_length):
    low_count = 64
    high = jnp.arange(nfft_length // low_count, dtype=jnp.int32) * low_count
    low = jnp.arange(low_count, dtype=jnp.int32)
    step = 2.0 * math.pi / nfft_length

    def waves(positions):
        phases = kept_channels[:, None] * positions[None, :] % nfft_length
        angles = phases.astype(jnp.float32) * step
        return jnp.cos(angles), jnp.sin(angles)

    high_cos, high_sin = waves(high)
    low_cos, low_sin = waves(low)
    expand = lambda x: jnp.repeat(x, low_count, axis=1)
    spread = lambda x: jnp.tile(x, (1, nfft_length // low_count))
    hc, hs, lc, ls = expand(high_cos), expand(high_sin), spread(low_cos), spread(low_sin)
    normalizer = 1.0 / math.sqrt(nfft_length)
    cosine = ((hc * lc - hs * ls) * normalizer).astype(jnp.bfloat16)
    sine = ((hs * lc + hc * ls) * normalizer).astype(jnp.bfloat16)
    return jnp.stack([jnp.stack([cosine, sine]), jnp.stack([-sine, cosine])])


def channelize_body(later, v_ref, c_ref, t_ref, out_ref, even, odd):
    step = pl.program_id(0)
    frames, inputs = v_ref.shape[1], v_ref.shape[2]
    taps = c_ref.shape[0]
    channels = t_ref.shape[2]
    width = v_ref.shape[3]
    pieces = inputs // GROUP
    piece = frames * GROUP

    def phase(filling, reading):
        def part(s, carry):
            row = pl.multiple_of(s * GROUP, GROUP)
            for p in range(2):
                for lane in range(0, width, LANES):
                    at = slice(lane, lane + LANES)
                    v = [
                        v_ref[p, f, pl.ds(row, GROUP), at].astype(jnp.float32)
                        for f in range(frames)
                    ]
                    c = [c_ref[t : t + 1, at] for t in range(taps)]
                    for f in range(frames):
                        total = None
                        for t in range(taps):
                            source = f - t + (frames if later else 0)
                            if 0 <= source < frames:
                                term = c[t] * v[source]
                                total = term if total is None else total + term
                        if total is None:
                            total = jnp.zeros((GROUP, LANES), jnp.float32)
                        upper = total.astype(jnp.bfloat16)
                        lower = (total - upper.astype(jnp.float32)).astype(jnp.bfloat16)
                        place = pl.ds(pl.multiple_of(f * inputs + row, GROUP), GROUP)
                        filling[2 * p, place, at] = upper
                        filling[2 * p + 1, place, at] = lower
            rows = pl.ds(pl.multiple_of(s * piece, LANES), piece)
            for h in range(2):
                total = None
                for p in range(2):
                    for q in range(2):
                        term = lax.dot_general(
                            t_ref[h, p],
                            reading[2 * p + q, rows, :],
                            (((1,), (1,)), ((), ())),
                            preferred_element_type=jnp.float32,
                        )
                        total = term if total is None else total + term
                before = out_ref[h, :, rows]
                out_ref[h, :, rows] = jnp.where(step <= 1, 0.0, before) + total
            return carry

        lax.fori_loop(0, pieces, part, 0)

    @pl.when(step % 2 == 0)
    def _():
        phase(even, odd)

    @pl.when(step % 2 == 1)
    def _():
        phase(odd, even)


def channelize(voltages, coefficients, blocks, later):
    _, frames, inputs, nfft_length = voltages.shape
    taps = coefficients.shape[0]
    channels = blocks.shape[2]
    rows = frames * inputs
    chunks = nfft_length // CHUNK
    last = chunks - 1
    return pl.pallas_call(
        lambda *refs: channelize_body(later, *refs),
        grid=(chunks + 1,),
        in_specs=[
            pl.BlockSpec((2, frames, inputs, CHUNK), lambda j: (0, 0, 0, jnp.minimum(j, last))),
            pl.BlockSpec((taps, CHUNK), lambda j: (0, jnp.minimum(j, last))),
            pl.BlockSpec((2, 2, channels, CHUNK), lambda j: (0, 0, 0, jnp.maximum(j - 1, 0))),
        ],
        out_specs=pl.BlockSpec((2, channels, rows), lambda j: (0, 0, 0)),
        out_shape=jax.ShapeDtypeStruct((2, channels, rows), jnp.float32),
        scratch_shapes=[pltpu.VMEM((4, rows, CHUNK), jnp.bfloat16)] * 2,
        compiler_params=pltpu.CompilerParams(vmem_limit_bytes=56 * 1024 * 1024),
        cost_estimate=pl.CostEstimate(
            flops=16 * rows * channels * nfft_length, bytes_accessed=60_000_000, transcendentals=0
        ),
    )(voltages, coefficients, blocks)


def correlate_body(scale, which_ref, s_ref, out_ref):
    n_time, n_station, _, count, frames, width = s_ref.shape
    inputs = out_ref.shape[2]
    groups = width // inputs
    which = which_ref[0]
    for k in range(count):
        parts = []
        for station in range(n_station):
            parts.append(
                jnp.concatenate(
                    [s_ref[t, station, p, k] for p in range(2) for t in range(n_time)], axis=0
                )
            )
        cuts = [
            parts[station][:, g * inputs : (g + 1) * inputs]
            for g in range(groups)
            for station in range(n_station)
        ]
        right = jnp.concatenate(cuts, axis=1)
        mine = cuts[0]
        for index in range(1, len(cuts)):
            mine = jnp.where(which == index, cuts[index], mine)
        half = mine.shape[0] // 2
        turned = jnp.concatenate([mine[half:], -mine[:half]], axis=0)
        for h, left in enumerate((mine, turned)):
            product = lax.dot_general(
                left, right, (((0,), (0,)), ((), ())), preferred_element_type=jnp.float32
            )
            out_ref[h, k] = product * scale


def correlate_part(everything, which, inputs, scale, owned, first, into):
    n_time, n_station, _, held, frames, width = everything.shape
    count = 4
    start = first // count
    more = [] if into is None else [into]
    total = n_station * width
    return pl.pallas_call(
        lambda *refs: correlate_body(scale, refs[0], refs[1], refs[-1]),
        grid=(held // count,),
        in_specs=[
            pl.BlockSpec(memory_space=pltpu.SMEM),
            pl.BlockSpec(
                (n_time, n_station, 2, count, frames, width), lambda j: (0, 0, 0, j, 0, 0)
            ),
        ]
        + [pl.BlockSpec(memory_space=pl.ANY) for _ in more],
        out_specs=pl.BlockSpec((2, count, inputs, total), lambda j: (0, j + start, 0, 0)),
        out_shape=jax.ShapeDtypeStruct((2, owned, inputs, total), jnp.float32),
        compiler_params=pltpu.CompilerParams(vmem_limit_bytes=48 * 1024 * 1024),
        input_output_aliases={2: 0} if more else {},
        cost_estimate=pl.CostEstimate(
            flops=500 * held * inputs * total,
            bytes_accessed=8 * held * inputs * total,
            transcendentals=0,
        ),
    )(which, everything, *more)


def shards(voltages, coefficients, kept_channels, station_flags):
    _, frames, inputs, nfft_length = voltages.shape
    channels = kept_channels.shape[0]
    n_time, n_station, n_chan = (lax.axis_size(a) for a in ("tm", "stn", "chan"))
    fits = (
        inputs % GROUP == 0
        and frames % 16 == 0
        and coefficients.shape[0] <= frames + 1
        and nfft_length % CHUNK == 0
        and frames * GROUP % LANES == 0
        and n_chan * n_station == n_time * n_station
        and n_chan * inputs % LANES == 0
        and channels // n_chan % 8 == 0
    )
    if not fits:
        return plain_shards(voltages, coefficients, kept_channels, station_flags)
    blocks = build_blocks(kept_channels, nfft_length)
    after = channelize(voltages, coefficients, blocks, True)
    earlier = passed_along(after, "tm", 1)
    own = channelize(voltages, coefficients, blocks, False)
    weights = jnp.tile(station_flags.astype(jnp.float32), frames)
    spectra = ((own + earlier) * weights).astype(jnp.bfloat16)
    owned = channels // n_chan
    spectra = spectra.reshape(2, n_chan, owned, frames, inputs)
    which = (lax.axis_index("tm") * n_station + lax.axis_index("stn")).astype(jnp.int32)[None]
    scale = 1.0 / (frames * n_time)
    half = owned // 2
    gathered = []
    for first in (0, half):
        sent = spectra[:, :, first : first + half]
        turned = lax.all_to_all(sent, "chan", split_axis=1, concat_axis=1, tiled=True)
        merged = jnp.transpose(turned, (0, 2, 3, 1, 4)).reshape(2, half, frames, n_chan * inputs)
        everything = lax.all_gather(merged[None], ("tm", "stn"), axis=0, tiled=True)
        gathered.append(everything.reshape(n_time, n_station, *merged.shape))
    result = correlate_part(gathered[0], which, inputs, scale, owned, 0, None)
    return correlate_part(gathered[1], which, inputs, scale, owned, half, result)


def solution(mesh):
    placed = (P(None, "tm", ("chan", "stn"), None), P(), P(), P(("chan", "stn")))
    return jax.shard_map(
        shards,
        mesh=mesh,
        in_specs=placed,
        out_specs=P(None, "chan", ("tm", "stn"), None),
        check_vma=False,
    )
```
